1024 devices in a mesh: space: 128 (over z, x), blk: 8 (over y, core).
Axes of the slice: x: 4, y: 4, z: 32, core: 2. Of those that a mesh axis runs over, the one named last changes fastest.
Arguments:
- snapshots: float32 [1024, 16, 16, 1024], P('space', None, None, 'blk'), may hold values from -40 to 40, as said below
Outputs:
- rotated: float32 [1024, 16, 16, 1024], P('space', None, None, 'blk')
The draws below stay inside these ranges and needn't reach their ends.
Inputs may be any that keep to these rules, and one draw needn't show every extreme that they name: `snapshots`: snapshot values are finite reals.
All inputs are finite; a program needn't handle non-finite values.
Results may differ from the reference program's by a relative error of at most 0.0003.
Values sent between devices are 32-bit elements; how exact they have to be, the bound alone decides.
A program may use at most 32 MiB of HBM per device.

```python
import jax
import jax.numpy as jnp
from jax import lax

GY = 16
GZ = 16
BLOCK = 128
ROUNDS = 2
NX = 1024
SNAPS = 1024
N_BLK = 8


def draw_snapshots(key, part):
    key_noise, key_class, key_shared, key_amp = jax.random.split(key, 4)
    shape = (NX, GY, GZ, SNAPS)
    classes = 8
    noise = jax.random.truncated_normal(key_noise, -4.0, 4.0, shape, jnp.float32)
    amps = jax.random.uniform(key_amp, (SNAPS,), jnp.float32, 0.5, 1.5)
    labels = jax.random.randint(key_class, (SNAPS,), 0, classes)
    shared = jax.random.truncated_normal(key_shared, -4.0, 4.0, (NX, GY, GZ, classes), jnp.float32)
    picked = jnp.take(shared, labels, axis=3)
    return (noise + amps * picked).astype(jnp.float32)


def setup_inputs(seed: int = 0) -> dict:
    key_of = jax.random.split(jax.random.key(seed), 2)
    return {
        "snapshots": draw_snapshots(jax.random.fold_in(key_of[1], 71), 0),
    }


def degree_field(size_x, size_y, size_z):
    pos_x = jnp.arange(size_x, dtype=jnp.int32)
    pos_y = jnp.arange(size_y, dtype=jnp.int32)
    pos_z = jnp.arange(size_z, dtype=jnp.int32)
    deg_x = (pos_x > 0).astype(jnp.float32) + (pos_x < size_x - 1).astype(jnp.float32)
    deg_y = (pos_y > 0).astype(jnp.float32) + (pos_y < size_y - 1).astype(jnp.float32)
    deg_z = (pos_z > 0).astype(jnp.float32) + (pos_z < size_z - 1).astype(jnp.float32)
    return deg_x[:, None, None] + deg_y[None, :, None] + deg_z[None, None, :]

def weighted(block, degree):
    padded = jnp.pad(block, ((1, 1), (1, 1), (1, 1), (0, 0)))
    near = padded[2:, 1:-1, 1:-1] + padded[:-2, 1:-1, 1:-1]
    near = near + padded[1:-1, 2:, 1:-1] + padded[1:-1, :-2, 1:-1]
    near = near + padded[1:-1, 1:-1, 2:] + padded[1:-1, 1:-1, :-2]
    return block + (degree[..., None] * block - near)

def gram_of(left, right):
    width = left.shape[-1]
    return lax.dot_general(left.reshape(-1, width).astype(jnp.float32), right.reshape(-1, width).astype(jnp.float32), (((0,), (0,)), ((), ())), precision=lax.Precision.HIGHEST, preferred_element_type=jnp.float32)

def rotation(own_diag, peer_diag, cross, parity):
    denom = jnp.diagonal(own_diag)[:, None] + jnp.diagonal(peer_diag)[None, :]
    ratios = cross / denom
    eye_mat = jnp.eye(cross.shape[0], dtype=jnp.float32)
    normal_mat = eye_mat + jnp.dot(ratios.astype(jnp.float32), ratios.T.astype(jnp.float32), precision=lax.Precision.HIGHEST, preferred_element_type=jnp.float32)
    factor = jnp.linalg.cholesky(normal_mat)
    inverse = jax.scipy.linalg.cho_solve((factor, True), eye_mat)
    solved = jax.scipy.linalg.cho_solve((factor, True), ratios)
    keep_mat = 2.0 * inverse - eye_mat
    take_mat = 2.0 * parity * solved.T
    return (keep_mat, take_mat)

def mix_blocks(own_block, peer_block, keep_mat, take_mat):
    width = own_block.shape[-1]
    first = jnp.dot(own_block.reshape(-1, width).astype(jnp.float32), keep_mat.astype(jnp.float32), precision=lax.Precision.HIGHEST, preferred_element_type=jnp.float32)
    second = jnp.dot(peer_block.reshape(-1, width).astype(jnp.float32), take_mat.astype(jnp.float32), precision=lax.Precision.HIGHEST, preferred_element_type=jnp.float32)
    return (first + second).reshape(own_block.shape)

def reference(snapshots):
    degree = degree_field(NX, GY, GZ)
    field = snapshots
    indices = jnp.arange(N_BLK, dtype=jnp.int32)
    for sweep_round in range(ROUNDS):

        def take_block(which):
            return lax.dynamic_slice_in_dim(field, (which * BLOCK).astype(jnp.int32), BLOCK, 3)

        def stats(which):
            own_block = take_block(which)
            peer_block = take_block(jnp.bitwise_xor(which, 1 << sweep_round))
            image = weighted(own_block, degree)
            return (gram_of(image, own_block), gram_of(image, peer_block))
        diag_all, cross_all = lax.map(stats, indices)

        def update(which):
            partner = jnp.bitwise_xor(which, 1 << sweep_round)
            parity = ((which >> sweep_round & 1) * 2 - 1).astype(jnp.float32)
            keep_mat, take_mat = rotation(diag_all[which], diag_all[partner], cross_all[which], parity)
            return mix_blocks(take_block(which), take_block(partner), keep_mat, take_mat)
        stacked = lax.map(update, indices)
        field = jnp.moveaxis(stacked, 0, 3).reshape(NX, GY, GZ, SNAPS)
    return field
```

```python
import functools

import jax
import jax.numpy as jnp
from jax import lax
from jax.experimental import pallas as pl
from jax.experimental.pallas import tpu as pltpu
from jax.sharding import PartitionSpec as P

ROUNDS = 2
NXC = 4
MESH = pl.DeviceIdType.MESH


def sum_kernel(nz, in_ref, out_ref, rx, part, rz, gz, send, recv):
    space = lax.axis_index("space")
    blk = lax.axis_index("blk")
    z, x = space // NXC, space % NXC
    rows = rx.shape[1]

    def x_peer(d):
        return z * NXC + (x + d) % NXC

    def z_peer(d):
        return ((z + d) % nz) * NXC + x

    def remote(src, dst, phase, peer):
        return pltpu.make_async_remote_copy(
            src_ref=src,
            dst_ref=dst,
            send_sem=send.at[phase],
            recv_sem=recv.at[phase],
            device_id=(peer, blk),
            device_id_type=MESH,
        )

    def wait_bytes(ref, phase):
        pltpu.make_async_copy(ref, ref, recv.at[phase]).wait()
        pltpu.make_async_copy(ref, ref, send.at[phase]).wait()

    barrier = pltpu.get_barrier_semaphore()
    for d in range(1, NXC):
        pl.semaphore_signal(barrier, inc=1, device_id=(x_peer(d), blk), device_id_type=MESH)

    @pl.loop(1, nz)
    def _(d):
        pl.semaphore_signal(barrier, inc=1, device_id=(z_peer(d), blk), device_id_type=MESH)

    pl.semaphore_wait(barrier, NXC - 1 + nz - 1)

    def own_rows(index):
        return pl.ds(pl.multiple_of(index * rows, rows), rows)

    for d in range(1, NXC):
        remote(in_ref.at[own_rows((x + d) % NXC)], rx.at[d - 1], 0, x_peer(d)).start()
    wait_bytes(rx, 0)
    mine = in_ref[own_rows(x)] + rx[0] + rx[1] + rx[2]
    part[...] = mine.reshape(part.shape)

    @pl.loop(1, nz)
    def _(d):
        remote(part.at[(z + d) % nz], rz.at[d - 1], 1, z_peer(d)).start()

    wait_bytes(rz, 1)
    gz[pl.ds(z, 1)] = part[pl.ds(z, 1)] + jnp.sum(rz[...], axis=0, keepdims=True)

    @pl.loop(1, nz)
    def _(d):
        remote(gz.at[z], gz.at[z], 2, z_peer(d)).start()

    wait_bytes(rz, 2)
    out_ref[own_rows(x)] = gz[...].reshape(rows, gz.shape[-1])
    for d in range(1, NXC):
        remote(out_ref.at[own_rows(x)], out_ref.at[own_rows(x)], 3, x_peer(d)).start()
    wait_bytes(rx, 3)


def sum_over_space(value):
    count = lax.axis_size("space")
    nz = count // NXC
    rows, cols = value.shape
    return pl.pallas_call(
        functools.partial(sum_kernel, nz),
        out_shape=jax.ShapeDtypeStruct(value.shape, value.dtype),
        in_specs=[pl.BlockSpec(memory_space=pltpu.VMEM)],
        out_specs=pl.BlockSpec(memory_space=pltpu.VMEM),
        scratch_shapes=[
            pltpu.VMEM((NXC - 1, rows // NXC, cols), jnp.float32),
            pltpu.VMEM((nz, rows // count, cols), jnp.float32),
            pltpu.VMEM((nz - 1, rows // count, cols), jnp.float32),
            pltpu.VMEM((nz, rows // count, cols), jnp.float32),
            pltpu.SemaphoreType.DMA((4,)),
            pltpu.SemaphoreType.DMA((4,)),
        ],
        compiler_params=pltpu.CompilerParams(collective_id=0, has_side_effects=True),
    )(value)


def padded_2(shard, sides, width):
    for axis, dim in sides:
        size, length = (lax.axis_size(axis), shard.shape[dim])
        up = [(i, (i + 1) % size) for i in range(size - 1)]
        down = [(j, i) for i, j in up]
        last = lax.slice_in_dim(shard, length - width, length, axis=dim)
        first = lax.slice_in_dim(shard, 0, width, axis=dim)
        before = lax.ppermute(last, axis, up)
        after = lax.ppermute(first, axis, down)
        shard = jnp.concatenate([before, shard, after], axis=dim)
    return shard


def from_partner(block, axis, stride):
    count = lax.axis_size(axis)
    route = []
    for low in range(count):
        high = low | 1 << stride
        if high != low and high < count:
            route += [(low, high), (high, low)]
    return lax.ppermute(block, axis, route)


def weighted(block):
    padded = padded_2(block, (("space", 0),), 1)
    layers = block.shape[0]
    cells_y = block.shape[1]
    cells_z = block.shape[2]
    sides = jnp.pad(block, ((0, 0), (1, 1), (1, 1), (0, 0)))
    near = padded[2:] + padded[:-2]
    near = near + sides[:, 2:, 1:-1] + sides[:, :-2, 1:-1]
    near = near + sides[:, 1:-1, 2:] + sides[:, 1:-1, :-2]
    total_x = layers * lax.axis_size("space")
    pos_x = lax.axis_index("space") * layers + jnp.arange(layers, dtype=jnp.int32)
    pos_y = jnp.arange(cells_y, dtype=jnp.int32)
    pos_z = jnp.arange(cells_z, dtype=jnp.int32)
    deg_x = (pos_x > 0).astype(jnp.float32) + (pos_x < total_x - 1).astype(jnp.float32)
    deg_y = (pos_y > 0).astype(jnp.float32) + (pos_y < cells_y - 1).astype(jnp.float32)
    deg_z = (pos_z > 0).astype(jnp.float32) + (pos_z < cells_z - 1).astype(jnp.float32)
    degree = deg_x[:, None, None] + deg_y[None, :, None] + deg_z[None, None, :]
    return block + (degree[..., None] * block - near)


def gram_of(left, right):
    width = left.shape[-1]
    return lax.dot_general(
        left.reshape(-1, width),
        right.reshape(-1, width),
        (((0,), (0,)), ((), ())),
        precision=lax.Precision.HIGHEST,
        preferred_element_type=jnp.float32,
    )


def rotation(own_diag, peer_diag, cross, parity):
    denom = jnp.diagonal(own_diag)[:, None] + jnp.diagonal(peer_diag)[None, :]
    ratios = cross / denom
    eye_mat = jnp.eye(cross.shape[0], dtype=jnp.float32)
    normal_mat = eye_mat + jnp.dot(
        ratios, ratios.T, precision=lax.Precision.HIGHEST, preferred_element_type=jnp.float32
    )
    factor = jnp.linalg.cholesky(normal_mat)
    inverse = jax.scipy.linalg.cho_solve((factor, True), eye_mat)
    solved = jax.scipy.linalg.cho_solve((factor, True), ratios)
    keep_mat = 2.0 * inverse - eye_mat
    take_mat = 2.0 * parity * solved.T
    return (keep_mat, take_mat)


def mix_blocks(own_block, peer_block, keep_mat, take_mat):
    width = own_block.shape[-1]
    first = jnp.dot(
        own_block.reshape(-1, width),
        keep_mat,
        precision=lax.Precision.HIGHEST,
        preferred_element_type=jnp.float32,
    )
    second = jnp.dot(
        peer_block.reshape(-1, width),
        take_mat,
        precision=lax.Precision.HIGHEST,
        preferred_element_type=jnp.float32,
    )
    return (first + second).reshape(own_block.shape)


def shards(snapshots):
    own_block = snapshots
    for sweep_round in range(ROUNDS):
        parity = ((lax.axis_index("blk") >> sweep_round & 1) * 2 - 1).astype(jnp.float32)
        outgoing = own_block
        incoming = from_partner(outgoing, "blk", sweep_round)
        image = weighted(own_block)
        local_diag = gram_of(image, own_block)
        local_cross = gram_of(image, incoming)
        total = sum_over_space(jnp.concatenate([local_diag, local_cross], axis=0))
        own_diag, cross = total[:128], total[128:]
        peer_diag = from_partner(own_diag, "blk", sweep_round)
        keep_mat, take_mat = rotation(own_diag, peer_diag, cross, parity)
        own_block = mix_blocks(own_block, incoming, keep_mat, take_mat)
    return own_block


def solution(mesh):
    return jax.shard_map(
        shards,
        mesh=mesh,
        in_specs=(P("space", None, None, "blk"),),
        out_specs=P("space", None, None, "blk"),
        check_vma=False,
    )
```

```python
import functools

import jax
import jax.numpy as jnp
from jax import lax
from jax.experimental import pallas as pl
from jax.experimental.pallas import tpu as pltpu
from jax.sharding import PartitionSpec as P

NXC = 4
GROUP = 4
BOX = 4
WIDTH = 128
F32, BF16 = jnp.float32, jnp.bfloat16
MESH = pl.DeviceIdType.MESH
ROWS_IN, ROWS_OUT = (((0,), (0,)), ((), ())), (((1,), (0,)), ((), ()))
LANES = (((1,), (1,)), ((), ()))
Z_IN = (-2, -1, 1)
Z_OUT = (-1, 1, 2)


def halves(value):
    high = value.astype(BF16)
    return high, (value - high.astype(F32)).astype(BF16)


def dot3(left, right, dims=ROWS_OUT):
    (lh, ll), (rh, rl) = left, right

    def dot(u, v):
        return lax.dot_general(u, v, dims, preferred_element_type=F32)

    return dot(lh, rh) + (dot(lh, rl) + dot(ll, rh))


def mul(left, right, dims=ROWS_OUT):
    return dot3(halves(left), halves(right), dims)


def eye_mask():
    shape = (WIDTH, WIDTH)
    return lax.broadcasted_iota(jnp.int32, shape, 0) == lax.broadcasted_iota(jnp.int32, shape, 1)


def inverse_of(matrix):
    panels = [matrix[8 * i : 8 * i + 8] for i in range(WIDTH // 8)]
    lane = lax.broadcasted_iota(jnp.int32, (8, WIDTH), 1)
    sub = lax.broadcasted_iota(jnp.int32, (8, WIDTH), 0)
    for k in range(WIDTH):
        home, s = k // 8, k % 8
        row = panels[home][s : s + 1]
        pivot = 1.0 / row[:, k : k + 1]
        row = jnp.where(lane[:1] == k, pivot, row * pivot)
        for i in range(len(panels)):
            old = panels[i]
            new = jnp.where(lane == k, 0.0, old) - old[:, k : k + 1] * row
            if i == home:
                new = jnp.where(sub == s, row, new)
            panels[i] = new
    return jnp.concatenate(panels, axis=0)


def rotation(own_col, peer_row, cross, parity):
    eye = jnp.where(eye_mask(), 1.0, 0.0)
    ratios = cross / (own_col + peer_row)
    inverse = inverse_of(eye + mul(ratios, ratios, LANES))
    solved = mul(inverse, ratios)
    return 2.0 * inverse - eye, (2.0 * parity) * solved.T


def kernel(nz, x_ref, out_ref, xp, xq, xq1, halo, w, wp, out_half, in_half, xh, xl, xph, xpl, wh, wl, first_h, first_l, bufs_a, bufs_b, core_a, keep_give, kt, ktq, send, recv):
    space, blk = lax.axis_index("space"), lax.axis_index("blk")
    count = nz * NXC
    z, x = space // NXC, space % NXC
    b4 = blk % GROUP
    base, low, high = blk - b4, b4 % 2, b4 // 2
    core = (space, base + 2 * high + 1 - low)
    peer_y = (space, base + (b4 + 2) % GROUP)
    after = ((space + 1) % count, blk)
    before = ((space + count - 1) % count, blk)
    layers = x_ref.shape[0]
    half = layers // 2

    def at(dz=0, dx=0, block=None):
        return (((z + dz + nz) % nz) * NXC + (x + dx) % NXC, blk if block is None else block)

    group = [at(0, g // GROUP, base + (b4 + g % GROUP) % GROUP) for g in range(1, NXC * GROUP)]
    rings = [at(dz) for dz in (-BOX, -2, -1, 1, 2, BOX)]

    copies = []

    def push(src, dst, device):
        index = len(copies)
        copy = pltpu.make_async_remote_copy(
            src_ref=src,
            dst_ref=dst,
            send_sem=send.at[index],
            recv_sem=recv.at[index],
            device_id=device,
            device_id_type=MESH,
        )
        copy.start()
        copies.append(copy)
        return copy

    def landed(*some):
        for copy in some:
            copy.wait_recv()

    barrier = pltpu.get_barrier_semaphore()
    peers = group + rings + [after, before]
    for device in peers:
        pl.semaphore_signal(barrier, inc=1, device_id=device, device_id_type=MESH)
    there, here = (1 - high) * half, high * half
    rows = x_ref.shape[1]
    side = rows // 16
    row = lax.broadcasted_iota(jnp.int32, (rows, WIDTH), 0)
    pos_y, pos_z = row // 16, row % 16

    def flag(cond):
        return jnp.where(cond, 1.0, 0.0)

    lowest, highest = flag(space > 0), flag(space < count - 1)
    plane = flag(pos_y > 0) + flag(pos_y < side - 1) + flag(pos_z > 0) + flag(pos_z < 15)
    zero16 = jnp.zeros((16, WIDTH), F32)

    def image(i, up, down, deg_x):
        cur = x_ref[i]
        near = up + down
        near = near + jnp.concatenate([cur[16:], zero16], axis=0)
        near = near + jnp.concatenate([zero16, cur[:-16]], axis=0)
        near = near + jnp.where(pos_z < 15, pltpu.roll(cur, rows - 1, 0), 0.0)
        near = near + jnp.where(pos_z > 0, pltpu.roll(cur, 1, 0), 0.0)
        value = cur + ((plane + deg_x) * cur - near)
        w[i] = value
        wh[i], wl[i] = halves(value)

    @pl.loop(1, layers - 1)
    def _(i):
        image(i, x_ref[i + 1], x_ref[i - 1], 2.0)

    def chunk(c):
        out_half[c] = jnp.where(high == 0, w[there + c], x_ref[there + c])
        return push(out_half.at[c], in_half.at[c], peer_y)

    pl.semaphore_wait(barrier, len(peers))
    chunks = [chunk(c) for c in range(half - 1)]
    halos = [push(x_ref.at[layers - 1], halo.at[0], after), push(x_ref.at[0], halo.at[1], before)]
    whole = push(x_ref, xp, core)

    @pl.loop(0, layers)
    def _(i):
        xh[i], xl[i] = halves(x_ref[i])

    landed(*halos)
    image(0, x_ref[1], jnp.where(space > 0, halo[0], 0.0), 1.0 + lowest)
    image(layers - 1, jnp.where(space < count - 1, halo[1], 0.0), x_ref[layers - 2], 1.0 + highest)
    chunks.append(chunk(half - 1))
    images = push(w.at[pl.ds(here, half)], wp, core)

    landed(whole)

    def gram_own(i, total):
        ph, plow = halves(xp[i])
        xph[i], xpl[i] = ph, plow
        right = (jnp.concatenate([xh[i], ph], axis=1), jnp.concatenate([xl[i], plow], axis=1))
        return total + dot3((wh[i], wl[i]), right, ROWS_IN)

    gram = lax.fori_loop(0, layers, gram_own, jnp.zeros((WIDTH, 2 * WIDTH), F32))
    ga, rxa, sa, rza, ringa, ta, gza, fa = bufs_a
    gb, rxb, sb, rzb, ringb, tb, gzb, fb = bufs_b
    for t in range(WIDTH // 8):
        ga[t // BOX, t % BOX, 0] = gram[8 * t : 8 * t + 8, :WIDTH]
        ga[t // BOX, t % BOX, 1] = gram[8 * t : 8 * t + 8, WIDTH:]

    def over_x(src, dst):
        return [push(src.at[(x + d) % NXC], dst.at[d - 1], at(0, d)) for d in range(1, NXC)]

    def over_z(src, dst):
        return [push(src.at[(z + o + nz) % BOX], dst.at[j], at(o)) for j, o in enumerate(Z_IN)]

    def ring_step(k, own, slots, boxes):
        up = boxes // 2
        out = [push(own if k == 0 else slots.at[k - 1], slots.at[k], at(BOX))]
        if k < boxes - 1 - up:
            out.append(push(own if k == 0 else slots.at[up + k - 1], slots.at[up + k], at(-BOX)))
        return out

    def back_z(src, dst):
        return [push(src, dst.at[z % BOX], at(o)) for o in Z_OUT]

    boxes = nz // BOX

    a_x = over_x(ga, rxa)
    landed(images)
    cross_own = jnp.zeros((WIDTH, WIDTH), F32)
    cross_peer = jnp.zeros((WIDTH, WIDTH), F32)
    a_z = None
    for c in range(half):
        landed(chunks[c])
        right = halves(in_half[c])
        own_left = halves(jnp.where(high == 0, w[here + c], x_ref[here + c]))
        peer_left = halves(jnp.where(high == 0, wp[c], xp[here + c]))
        cross_own = cross_own + dot3(own_left, right, ROWS_IN)
        cross_peer = cross_peer + dot3(peer_left, right, ROWS_IN)
        if c == half // 2 - 1:
            landed(*a_x)
            sa[...] = ga[x] + rxa[0] + rxa[1] + rxa[2]
            a_z = over_z(sa, rza)
    keep = jnp.where(high == 0, cross_own, cross_peer.T)
    give = jnp.where(high == 0, cross_peer, cross_own.T)
    for t in range(WIDTH // 8):
        gb[t // BOX, t % BOX] = keep[8 * t : 8 * t + 8]
        keep_give[t // BOX, t % BOX] = give[8 * t : 8 * t + 8]
    owner = base + (1 - high) * (3 - b4) + high * (b4 - 2)
    b_x = over_x(gb, rxb)
    b_x += [push(keep_give.at[(x + d) % NXC], rxb.at[3 + d], at(0, d, owner)) for d in range(NXC)]
    rest = push(x_ref, xq, peer_y)

    landed(*a_z)
    ta[...] = sa[z % BOX] + rza[0] + rza[1] + rza[2]
    a_r = ring_step(0, ta, ringa, boxes)
    landed(*b_x)
    total = gb[x]
    for j in range(7):
        total = total + rxb[j]
    sb[...] = total
    b_z = over_z(sb, rzb)
    steps = boxes // 2
    landed(*a_r)
    a_r = ring_step(1, ta, ringa, boxes)
    landed(*b_z)
    tb[...] = sb[z % BOX] + rzb[0] + rzb[1] + rzb[2]
    b_r = ring_step(0, tb, ringb, boxes)
    for k in range(2, steps):
        landed(*a_r)
        a_r = ring_step(k, ta, ringa, boxes)
        landed(*b_r)
        b_r = ring_step(k - 1, tb, ringb, boxes)
    landed(*a_r)
    total = ta[...]
    for j in range(boxes - 1):
        total = total + ringa[j]
    gza[z % BOX] = total
    a_g = back_z(gza.at[z % BOX], gza)
    landed(*b_r)
    b_r = ring_step(steps - 1, tb, ringb, boxes)
    landed(*a_g)
    fa[x] = gza[...]
    a_g = [push(fa.at[x], fa.at[x], at(0, d)) for d in range(1, NXC)]
    landed(*b_r)
    total = tb[...]
    for j in range(boxes - 1):
        total = total + ringb[j]
    gzb[z % BOX] = total
    b_g = back_z(gzb.at[z % BOX], gzb)
    landed(*a_g)
    a_c = push(fa, core_a, core)
    landed(*b_g)
    fb[b4, x] = gzb[...]
    b_g = [push(fb.at[b4, x], fb.at[b4, x], device) for device in group]

    landed(rest)
    forward = push(xq, xq1, core)
    landed(a_c)
    square = (WIDTH, WIDTH)
    own_a, own_c = fa[:, :, 0].reshape(square), fa[:, :, 1].reshape(square)
    peer_a, peer_c = core_a[:, :, 0].reshape(square), core_a[:, :, 1].reshape(square)
    eye = eye_mask()

    def column(values):
        return jnp.sum(jnp.where(eye, values, 0.0), axis=1, keepdims=True)

    def diag_row(values):
        return jnp.sum(jnp.where(eye, values, 0.0), axis=0, keepdims=True)

    keep_m, take_m = rotation(column(own_a), diag_row(peer_a), own_c, jnp.where(low == 1, 1.0, -1.0))
    pair = jnp.concatenate([keep_m, take_m], axis=0)
    full = jnp.concatenate(
        [jnp.concatenate([own_a, own_c], axis=1), jnp.concatenate([peer_c, peer_a], axis=1)], axis=0
    )
    own_diag = jnp.sum(pair * mul(full, pair), axis=0, keepdims=True)
    kt[: 2 * WIDTH] = pair
    kt[2 * WIDTH :] = jnp.broadcast_to(own_diag, (8, WIDTH))
    turn = push(kt, ktq, peer_y)

    def wide(pair):
        ph, plow = halves(pair)
        return jnp.concatenate([ph, plow], axis=1), ph

    def mixed(lh, ll, right):
        both, ph = right
        part = lax.dot_general(lh, both, ROWS_OUT, preferred_element_type=F32)
        last = lax.dot_general(ll, ph, ROWS_OUT, preferred_element_type=F32)
        return part[:, :WIDTH] + (part[:, WIDTH:] + last)

    own_wide = wide(pair)

    @pl.loop(0, layers)
    def _(i):
        lh = jnp.concatenate([xh[i], xph[i]], axis=1)
        ll = jnp.concatenate([xl[i], xpl[i]], axis=1)
        first_h[i, :, :WIDTH], first_l[i, :, :WIDTH] = halves(mixed(lh, ll, own_wide))

    landed(forward, turn)
    pair_q = ktq[: 2 * WIDTH]
    diag_q = ktq[2 * WIDTH : 2 * WIDTH + 1]
    peer_wide = wide(pair_q)

    @pl.loop(0, layers)
    def _(i):
        qh, ql = halves(xq[i])
        q1h, q1l = halves(xq1[i])
        lh, ll = jnp.concatenate([qh, q1h], axis=1), jnp.concatenate([ql, q1l], axis=1)
        first_h[i, :, WIDTH:], first_l[i, :, WIDTH:] = halves(mixed(lh, ll, peer_wide))

    landed(*b_g)
    top = jnp.concatenate([fb[low].reshape(square), fb[2 + low].reshape(square)], axis=1)
    bottom = jnp.concatenate([fb[3 - low].reshape(square), fb[1 - low].reshape(square)], axis=1)
    cross = jnp.concatenate([top, bottom], axis=0)
    left = jnp.where(high == 0, pair, pair_q)
    right = jnp.where(high == 0, pair_q, pair)
    turned = mul(left, mul(cross, right), ROWS_IN)
    turned = jnp.where(high == 0, turned, turned.T)
    keep_m, take_m = rotation(column(own_diag), diag_q, turned, jnp.where(high == 1, 1.0, -1.0))
    last_wide = wide(jnp.concatenate([keep_m, take_m], axis=0))

    @pl.loop(0, layers)
    def _(i):
        out_ref[i] = mixed(first_h[i], first_l[i], last_wide)

    for copy in copies:
        copy.wait_send()


def rotate(block):
    nz = lax.axis_size("space") // NXC
    layers, rows, _ = block.shape
    half = layers // 2
    boxes = nz // BOX
    full = pltpu.VMEM((layers, rows, WIDTH), F32)
    part = pltpu.VMEM((layers, rows, WIDTH), BF16)
    double = pltpu.VMEM((layers, rows, 2 * WIDTH), BF16)

    def sums(arrivals, trail, blocks):
        return [
            pltpu.VMEM((NXC, BOX) + trail, F32),
            pltpu.VMEM((arrivals, BOX) + trail, F32),
            pltpu.VMEM((BOX,) + trail, F32),
            pltpu.VMEM((3,) + trail, F32),
            pltpu.VMEM((boxes - 1,) + trail, F32),
            pltpu.VMEM(trail, F32),
            pltpu.VMEM((BOX,) + trail, F32),
            pltpu.VMEM(blocks + (NXC, BOX) + trail, F32),
        ]

    trail_a, trail_b = (2, 8, WIDTH), (8, WIDTH)
    return pl.pallas_call(
        functools.partial(kernel, nz),
        out_shape=jax.ShapeDtypeStruct(block.shape, F32),
        in_specs=[pl.BlockSpec(memory_space=pltpu.VMEM)],
        out_specs=pl.BlockSpec(memory_space=pltpu.VMEM),
        scratch_shapes=[
            full,
            full,
            full,
            pltpu.VMEM((2, rows, WIDTH), F32),
            full,
            pltpu.VMEM((half, rows, WIDTH), F32),
            pltpu.VMEM((half, rows, WIDTH), F32),
            pltpu.VMEM((half, rows, WIDTH), F32),
            part,
            part,
            part,
            part,
            part,
            part,
            double,
            double,
            sums(3, trail_a, ()),
            sums(7, trail_b, (GROUP,)),
            pltpu.VMEM((NXC, BOX) + trail_a, F32),
            pltpu.VMEM((NXC, BOX) + trail_b, F32),
            pltpu.VMEM((2 * WIDTH + 8, WIDTH), F32),
            pltpu.VMEM((2 * WIDTH + 8, WIDTH), F32),
            pltpu.SemaphoreType.DMA((80,)),
            pltpu.SemaphoreType.DMA((80,)),
        ],
        compiler_params=pltpu.CompilerParams(
            collective_id=0, has_side_effects=True, vmem_limit_bytes=48 * 1024 * 1024
        ),
    )(block)


def shards(snapshots):
    layers, cells_y, cells_z, width = snapshots.shape
    return rotate(snapshots.reshape(layers, cells_y * cells_z, width)).reshape(snapshots.shape)


def solution(mesh):
    return jax.shard_map(
        shards,
        mesh=mesh,
        in_specs=(P("space", None, None, "blk"),),
        out_specs=P("space", None, None, "blk"),
        check_vma=False,
    )
```

```python
import functools

import jax
import jax.numpy as jnp
from jax import lax
from jax.experimental import pallas as pl
from jax.experimental.pallas import tpu as pltpu
from jax.sharding import PartitionSpec as P

NXC = 4
GROUP = 4
BOX = 4
WIDTH = 128
F32, BF16 = jnp.float32, jnp.bfloat16
MESH = pl.DeviceIdType.MESH
ROWS_IN, ROWS_OUT = (((0,), (0,)), ((), ())), (((1,), (0,)), ((), ()))
LANES = (((1,), (1,)), ((), ()))
Z_IN = (-2, -1, 1)
Z_OUT = (-1, 1, 2)


def halves(value):
    high = value.astype(BF16)
    return high, (value - high.astype(F32)).astype(BF16)


def dot3(left, right, dims=ROWS_OUT):
    (lh, ll), (rh, rl) = left, right

    def dot(u, v):
        return lax.dot_general(u, v, dims, preferred_element_type=F32)

    return dot(lh, rh) + (dot(lh, rl) + dot(ll, rh))


def mul(left, right, dims=ROWS_OUT):
    return dot3(halves(left), halves(right), dims)


def eye_mask():
    shape = (WIDTH, WIDTH)
    return lax.broadcasted_iota(jnp.int32, shape, 0) == lax.broadcasted_iota(jnp.int32, shape, 1)


def inverse_of(matrix, between):
    count = WIDTH // 8
    shape = (8, WIDTH)
    panels = [matrix[8 * i : 8 * i + 8] for i in range(count)]
    lane = lax.broadcasted_iota(jnp.int32, shape, 1)
    sub = lax.broadcasted_iota(jnp.int32, shape, 0)
    for home in range(count):
        first = 8 * home
        rows = [jnp.broadcast_to(panels[home][t : t + 1], shape) for t in range(8)]
        entry = [[None] * 8 for _ in range(8)]
        for t in range(8):
            for u in range(t, 8):
                place = rows[t][:, first + u : first + u + 1]
                entry[t][u] = entry[u][t] = jnp.broadcast_to(place, shape)
        block = (lane >= first) & (lane < first + 8)
        for t in range(8):
            rows[t] = jnp.where(block, jnp.where(lane == first + t, 1.0, 0.0), rows[t])
        for t in range(8):
            pivot = 1.0 / entry[t][t]
            rows[t] = rows[t] * pivot
            for v in range(t + 1, 8):
                entry[t][v] = entry[t][v] * pivot
            for u in range(8):
                if u != t:
                    rows[u] = rows[u] - entry[u][t] * rows[t]
                    for v in range(t + 1, 8):
                        entry[u][v] = entry[u][v] - entry[u][t] * entry[t][v]
        for i in range(count):
            old = panels[i]
            if i == home:
                new = rows[0]
                for t in range(1, 8):
                    new = jnp.where(sub == t, rows[t], new)
            else:
                new = jnp.where(block, 0.0, old)
                for t in range(8):
                    new = new - old[:, first + t : first + t + 1] * rows[t]
            panels[i] = new
        between(home)
    return jnp.concatenate(panels, axis=0)


def rotation(own_col, peer_row, cross, parity, between):
    eye = jnp.where(eye_mask(), 1.0, 0.0)
    ratios = cross / (own_col + peer_row)
    inverse = inverse_of(eye + mul(ratios, ratios, LANES), between)
    solved = mul(inverse, ratios)
    return 2.0 * inverse - eye, (2.0 * parity) * solved.T


def kernel(nz, x_ref, out_ref, xp, xq, xq1, halo, w, wp, out_half, in_half, xh, xl, xph, xpl, wh, wl, first_h, first_l, bufs_a, bufs_b, core_a, keep_give, kt, ktq, send, recv):
    space, blk = lax.axis_index("space"), lax.axis_index("blk")
    count = nz * NXC
    z, x = space // NXC, space % NXC
    b4 = blk % GROUP
    base, low, high = blk - b4, b4 % 2, b4 // 2
    core = (space, base + 2 * high + 1 - low)
    peer_y = (space, base + (b4 + 2) % GROUP)
    after = ((space + 1) % count, blk)
    before = ((space + count - 1) % count, blk)
    layers = x_ref.shape[0]
    half = layers // 2

    def at(dz=0, dx=0, block=None):
        return (((z + dz + nz) % nz) * NXC + (x + dx) % NXC, blk if block is None else block)

    group = [at(0, g // GROUP, base + (b4 + g % GROUP) % GROUP) for g in range(1, NXC * GROUP)]
    rings = [at(dz) for dz in (-BOX, -2, -1, 1, 2, BOX)]

    copies = []

    def push(src, dst, device):
        index = len(copies)
        copy = pltpu.make_async_remote_copy(
            src_ref=src,
            dst_ref=dst,
            send_sem=send.at[index],
            recv_sem=recv.at[index],
            device_id=device,
            device_id_type=MESH,
        )
        copy.start()
        copies.append(copy)
        return copy

    def landed(*some):
        for copy in some:
            copy.wait_recv()

    barrier = pltpu.get_barrier_semaphore()
    peers = group + rings + [after, before]
    for device in peers:
        pl.semaphore_signal(barrier, inc=1, device_id=device, device_id_type=MESH)
    there, here = (1 - high) * half, high * half
    rows = x_ref.shape[1]
    side = rows // 16
    row = lax.broadcasted_iota(jnp.int32, (rows, WIDTH), 0)
    pos_y, pos_z = row // 16, row % 16

    def flag(cond):
        return jnp.where(cond, 1.0, 0.0)

    lowest, highest = flag(space > 0), flag(space < count - 1)
    plane = flag(pos_y > 0) + flag(pos_y < side - 1) + flag(pos_z > 0) + flag(pos_z < 15)
    zero16 = jnp.zeros((16, WIDTH), F32)

    def image(i, up, down, deg_x):
        cur = x_ref[i]
        near = up + down
        near = near + jnp.concatenate([cur[16:], zero16], axis=0)
        near = near + jnp.concatenate([zero16, cur[:-16]], axis=0)
        near = near + jnp.where(pos_z < 15, pltpu.roll(cur, rows - 1, 0), 0.0)
        near = near + jnp.where(pos_z > 0, pltpu.roll(cur, 1, 0), 0.0)
        value = cur + ((plane + deg_x) * cur - near)
        w[i] = value
        wh[i], wl[i] = halves(value)

    @pl.loop(1, layers - 1)
    def _(i):
        image(i, x_ref[i + 1], x_ref[i - 1], 2.0)

    def chunk(c):
        out_half[c] = jnp.where(high == 0, w[there + c], x_ref[there + c])
        return push(out_half.at[c], in_half.at[c], peer_y)

    pl.semaphore_wait(barrier, len(peers))
    chunks = [chunk(c) for c in range(half - 1)]
    halos = [push(x_ref.at[layers - 1], halo.at[0], after), push(x_ref.at[0], halo.at[1], before)]
    whole = push(x_ref, xp, core)

    @pl.loop(0, layers)
    def _(i):
        xh[i], xl[i] = halves(x_ref[i])

    landed(*halos)
    image(0, x_ref[1], jnp.where(space > 0, halo[0], 0.0), 1.0 + lowest)
    image(layers - 1, jnp.where(space < count - 1, halo[1], 0.0), x_ref[layers - 2], 1.0 + highest)
    chunks.append(chunk(half - 1))
    images = push(w.at[pl.ds(here, half)], wp, core)

    landed(whole)

    def gram_own(i, total):
        ph, plow = halves(xp[i])
        xph[i], xpl[i] = ph, plow
        right = (jnp.concatenate([xh[i], ph], axis=1), jnp.concatenate([xl[i], plow], axis=1))
        return total + dot3((wh[i], wl[i]), right, ROWS_IN)

    gram = lax.fori_loop(0, layers, gram_own, jnp.zeros((WIDTH, 2 * WIDTH), F32))
    ga, rxa, sa, rza, ringa, ta, gza, fa = bufs_a
    gb, rxb, sb, rzb, ringb, tb, gzb, fb = bufs_b
    for t in range(WIDTH // 8):
        ga[t // BOX, t % BOX, 0] = gram[8 * t : 8 * t + 8, :WIDTH]
        ga[t // BOX, t % BOX, 1] = gram[8 * t : 8 * t + 8, WIDTH:]

    def over_x(src, dst):
        return [push(src.at[(x + d) % NXC], dst.at[d - 1], at(0, d)) for d in range(1, NXC)]

    def over_z(src, dst):
        return [push(src.at[(z + o + nz) % BOX], dst.at[j], at(o)) for j, o in enumerate(Z_IN)]

    def ring_step(k, own, slots, boxes):
        up = boxes // 2
        out = [push(own if k == 0 else slots.at[k - 1], slots.at[k], at(BOX))]
        if k < boxes - 1 - up:
            out.append(push(own if k == 0 else slots.at[up + k - 1], slots.at[up + k], at(-BOX)))
        return out

    def back_z(src, dst):
        return [push(src, dst.at[z % BOX], at(o)) for o in Z_OUT]

    boxes = nz // BOX

    a_x = over_x(ga, rxa)
    landed(images)
    cross_own = jnp.zeros((WIDTH, WIDTH), F32)
    cross_peer = jnp.zeros((WIDTH, WIDTH), F32)
    a_z = None
    a_r = None
    for c in range(half):
        landed(chunks[c])
        right = halves(in_half[c])
        own_left = halves(jnp.where(high == 0, w[here + c], x_ref[here + c]))
        peer_left = halves(jnp.where(high == 0, wp[c], xp[here + c]))
        cross_own = cross_own + dot3(own_left, right, ROWS_IN)
        cross_peer = cross_peer + dot3(peer_left, right, ROWS_IN)
        if c == 0:
            landed(*a_x)
            sa[...] = ga[x] + rxa[0] + rxa[1] + rxa[2]
            a_z = over_z(sa, rza)
        if c == half - 2:
            landed(*a_z)
            ta[...] = sa[z % BOX] + rza[0] + rza[1] + rza[2]
            a_r = ring_step(0, ta, ringa, boxes)
    keep = jnp.where(high == 0, cross_own, cross_peer.T)
    give = jnp.where(high == 0, cross_peer, cross_own.T)
    for t in range(WIDTH // 8):
        gb[t // BOX, t % BOX] = keep[8 * t : 8 * t + 8]
        keep_give[t // BOX, t % BOX] = give[8 * t : 8 * t + 8]
    owner = base + (1 - high) * (3 - b4) + high * (b4 - 2)
    b_x = over_x(gb, rxb)
    b_x += [push(keep_give.at[(x + d) % NXC], rxb.at[3 + d], at(0, d, owner)) for d in range(NXC)]
    rest = push(x_ref, xq, peer_y)

    steps = boxes // 2
    landed(*a_r)
    a_r = ring_step(1, ta, ringa, boxes)
    landed(*b_x)
    total = gb[x]
    for j in range(7):
        total = total + rxb[j]
    sb[...] = total
    b_z = over_z(sb, rzb)
    landed(*a_r)
    a_r = ring_step(2, ta, ringa, boxes)
    landed(*b_z)
    tb[...] = sb[z % BOX] + rzb[0] + rzb[1] + rzb[2]
    b_r = ring_step(0, tb, ringb, boxes)
    landed(*a_r)
    a_r = ring_step(3, ta, ringa, boxes)
    landed(*b_r)
    b_r = ring_step(1, tb, ringb, boxes)
    landed(*a_r)
    total = ta[...]
    for j in range(boxes - 1):
        total = total + ringa[j]
    gza[z % BOX] = total
    a_g = back_z(gza.at[z % BOX], gza)
    landed(*b_r)
    b_r = ring_step(2, tb, ringb, boxes)
    landed(*a_g)
    fa[x] = gza[...]
    a_g = [push(fa.at[x], fa.at[x], at(0, d)) for d in range(1, NXC)]
    landed(*b_r)
    b_r = ring_step(3, tb, ringb, boxes)
    landed(*a_g)
    a_c = push(fa, core_a, core)
    landed(*b_r)
    total = tb[...]
    for j in range(boxes - 1):
        total = total + ringb[j]
    gzb[z % BOX] = total
    b_g = back_z(gzb.at[z % BOX], gzb)
    landed(a_c)
    square = (WIDTH, WIDTH)
    own_a, own_c = fa[:, :, 0].reshape(square), fa[:, :, 1].reshape(square)
    peer_a, peer_c = core_a[:, :, 0].reshape(square), core_a[:, :, 1].reshape(square)
    eye = eye_mask()

    def column(values):
        return jnp.sum(jnp.where(eye, values, 0.0), axis=1, keepdims=True)

    def diag_row(values):
        return jnp.sum(jnp.where(eye, values, 0.0), axis=0, keepdims=True)

    spread, moved = [], []

    def serve(step):
        if step == 6:
            landed(*b_g)
            fb[b4, x] = gzb[...]
            spread.extend(push(fb.at[b4, x], fb.at[b4, x], device) for device in group)
        if step == 11:
            landed(rest)
            moved.append(push(xq, xq1, core))

    sign = jnp.where(low == 1, 1.0, -1.0)
    keep_m, take_m = rotation(column(own_a), diag_row(peer_a), own_c, sign, serve)
    pair = jnp.concatenate([keep_m, take_m], axis=0)
    full = jnp.concatenate(
        [jnp.concatenate([own_a, own_c], axis=1), jnp.concatenate([peer_c, peer_a], axis=1)], axis=0
    )
    own_diag = jnp.sum(pair * mul(full, pair), axis=0, keepdims=True)
    kt[: 2 * WIDTH] = pair
    kt[2 * WIDTH :] = jnp.broadcast_to(own_diag, (8, WIDTH))
    turn = push(kt, ktq, peer_y)

    def wide(pair):
        ph, plow = halves(pair)
        return jnp.concatenate([ph, plow], axis=1), ph

    def mixed(lh, ll, right):
        both, ph = right
        part = lax.dot_general(lh, both, ROWS_OUT, preferred_element_type=F32)
        last = lax.dot_general(ll, ph, ROWS_OUT, preferred_element_type=F32)
        return part[:, :WIDTH] + (part[:, WIDTH:] + last)

    own_wide = wide(pair)
    landed(turn)
    pair_q = ktq[: 2 * WIDTH]
    diag_q = ktq[2 * WIDTH : 2 * WIDTH + 1]
    peer_wide = wide(pair_q)
    landed(*spread)
    top = jnp.concatenate([fb[low].reshape(square), fb[2 + low].reshape(square)], axis=1)
    bottom = jnp.concatenate([fb[3 - low].reshape(square), fb[1 - low].reshape(square)], axis=1)
    cross = jnp.concatenate([top, bottom], axis=0)
    left = jnp.where(high == 0, pair, pair_q)
    right = jnp.where(high == 0, pair_q, pair)
    turned = mul(left, mul(cross, right), ROWS_IN)
    turned = jnp.where(high == 0, turned, turned.T)
    landed(*moved)

    def first_round(step):
        i = step // 2
        if step % 2 == 0:
            lh = jnp.concatenate([xh[i], xph[i]], axis=1)
            ll = jnp.concatenate([xl[i], xpl[i]], axis=1)
            first_h[i, :, :WIDTH], first_l[i, :, :WIDTH] = halves(mixed(lh, ll, own_wide))
        else:
            qh, ql = halves(xq[i])
            q1h, q1l = halves(xq1[i])
            lh, ll = jnp.concatenate([qh, q1h], axis=1), jnp.concatenate([ql, q1l], axis=1)
            first_h[i, :, WIDTH:], first_l[i, :, WIDTH:] = halves(mixed(lh, ll, peer_wide))

    sign = jnp.where(high == 1, 1.0, -1.0)
    keep_m, take_m = rotation(column(own_diag), diag_q, turned, sign, first_round)
    last_wide = wide(jnp.concatenate([keep_m, take_m], axis=0))

    @pl.loop(0, layers)
    def _(i):
        out_ref[i] = mixed(first_h[i], first_l[i], last_wide)

    for copy in copies:
        copy.wait_send()


def rotate(block):
    nz = lax.axis_size("space") // NXC
    layers, rows, _ = block.shape
    half = layers // 2
    boxes = nz // BOX
    full = pltpu.VMEM((layers, rows, WIDTH), F32)
    part = pltpu.VMEM((layers, rows, WIDTH), BF16)
    double = pltpu.VMEM((layers, rows, 2 * WIDTH), BF16)

    def sums(arrivals, trail, blocks):
        return [
            pltpu.VMEM((NXC, BOX) + trail, F32),
            pltpu.VMEM((arrivals, BOX) + trail, F32),
            pltpu.VMEM((BOX,) + trail, F32),
            pltpu.VMEM((3,) + trail, F32),
            pltpu.VMEM((boxes - 1,) + trail, F32),
            pltpu.VMEM(trail, F32),
            pltpu.VMEM((BOX,) + trail, F32),
            pltpu.VMEM(blocks + (NXC, BOX) + trail, F32),
        ]

    trail_a, trail_b = (2, 8, WIDTH), (8, WIDTH)
    return pl.pallas_call(
        functools.partial(kernel, nz),
        out_shape=jax.ShapeDtypeStruct(block.shape, F32),
        in_specs=[pl.BlockSpec(memory_space=pltpu.VMEM)],
        out_specs=pl.BlockSpec(memory_space=pltpu.VMEM),
        scratch_shapes=[
            full,
            full,
            full,
            pltpu.VMEM((2, rows, WIDTH), F32),
            full,
            pltpu.VMEM((half, rows, WIDTH), F32),
            pltpu.VMEM((half, rows, WIDTH), F32),
            pltpu.VMEM((half, rows, WIDTH), F32),
            part,
            part,
            part,
            part,
            part,
            part,
            double,
            double,
            sums(3, trail_a, ()),
            sums(7, trail_b, (GROUP,)),
            pltpu.VMEM((NXC, BOX) + trail_a, F32),
            pltpu.VMEM((NXC, BOX) + trail_b, F32),
            pltpu.VMEM((2 * WIDTH + 8, WIDTH), F32),
            pltpu.VMEM((2 * WIDTH + 8, WIDTH), F32),
            pltpu.SemaphoreType.DMA((80,)),
            pltpu.SemaphoreType.DMA((80,)),
        ],
        compiler_params=pltpu.CompilerParams(
            collective_id=0, has_side_effects=True, vmem_limit_bytes=48 * 1024 * 1024
        ),
    )(block)


def shards(snapshots):
    layers, cells_y, cells_z, width = snapshots.shape
    return rotate(snapshots.reshape(layers, cells_y * cells_z, width)).reshape(snapshots.shape)


def solution(mesh):
    return jax.shard_map(
        shards,
        mesh=mesh,
        in_specs=(P("space", None, None, "blk"),),
        out_specs=P("space", None, None, "blk"),
        check_vma=False,
    )
```

```python
import functools

import jax
import jax.numpy as jnp
from jax import lax
from jax.experimental import pallas as pl
from jax.experimental.pallas import tpu as pltpu
from jax.sharding import PartitionSpec as P

NXC = 4
GROUP = 4
BOX = 4
WIDTH = 128
F32, BF16 = jnp.float32, jnp.bfloat16
MESH = pl.DeviceIdType.MESH
ROWS_IN, ROWS_OUT = (((0,), (0,)), ((), ())), (((1,), (0,)), ((), ()))
LANES = (((1,), (1,)), ((), ()))
Z_IN = (-2, -1, 1)
Z_OUT = (-1, 1, 2)


def halves(value):
    high = value.astype(BF16)
    return high, (value - high.astype(F32)).astype(BF16)


def dot3(left, right, dims=ROWS_OUT):
    (lh, ll), (rh, rl) = left, right

    def dot(u, v):
        return lax.dot_general(u, v, dims, preferred_element_type=F32)

    return dot(lh, rh) + (dot(lh, rl) + dot(ll, rh))


def mul(left, right, dims=ROWS_OUT):
    return dot3(halves(left), halves(right), dims)


def eye_mask():
    shape = (WIDTH, WIDTH)
    return lax.broadcasted_iota(jnp.int32, shape, 0) == lax.broadcasted_iota(jnp.int32, shape, 1)


def inverse_of(matrix, between):
    count = WIDTH // 8
    shape = (8, WIDTH)
    panels = [matrix[8 * i : 8 * i + 8] for i in range(count)]
    lane = lax.broadcasted_iota(jnp.int32, shape, 1)
    sub = lax.broadcasted_iota(jnp.int32, shape, 0)
    for home in range(count):
        first = 8 * home
        rows = [jnp.broadcast_to(panels[home][t : t + 1], shape) for t in range(8)]
        entry = [[None] * 8 for _ in range(8)]
        for t in range(8):
            for u in range(t, 8):
                place = rows[t][:, first + u : first + u + 1]
                entry[t][u] = entry[u][t] = jnp.broadcast_to(place, shape)
        block = (lane >= first) & (lane < first + 8)
        for t in range(8):
            rows[t] = jnp.where(block, jnp.where(lane == first + t, 1.0, 0.0), rows[t])
        for t in range(8):
            pivot = 1.0 / entry[t][t]
            rows[t] = rows[t] * pivot
            for v in range(t + 1, 8):
                entry[t][v] = entry[t][v] * pivot
            for u in range(8):
                if u != t:
                    rows[u] = rows[u] - entry[u][t] * rows[t]
                    for v in range(t + 1, 8):
                        entry[u][v] = entry[u][v] - entry[u][t] * entry[t][v]
        for i in range(count):
            old = panels[i]
            if i == home:
                new = rows[0]
                for t in range(1, 8):
                    new = jnp.where(sub == t, rows[t], new)
            else:
                new = jnp.where(block, 0.0, old)
                for t in range(8):
                    new = new - old[:, first + t : first + t + 1] * rows[t]
            panels[i] = new
        between(home)
    return jnp.concatenate(panels, axis=0)


def rotation(own_col, peer_row, cross, parity, between):
    eye = jnp.where(eye_mask(), 1.0, 0.0)
    ratios = cross / (own_col + peer_row)
    inverse = inverse_of(eye + mul(ratios, ratios, LANES), between)
    solved = mul(inverse, ratios)
    return 2.0 * inverse - eye, (2.0 * parity) * solved.T


def kernel(nz, x_ref, out_ref, xp, xq, xq1, halo, w, wp, out_half, in_half, xh, xl, xph, xpl, wh, wl, first_h, first_l, bufs_a, bufs_b, core_a, keep_give, kt, ktq, dg, dgq, send, recv):
    space, blk = lax.axis_index("space"), lax.axis_index("blk")
    count = nz * NXC
    z, x = space // NXC, space % NXC
    b4 = blk % GROUP
    base, low, high = blk - b4, b4 % 2, b4 // 2
    core = (space, base + 2 * high + 1 - low)
    peer_y = (space, base + (b4 + 2) % GROUP)
    after = ((space + 1) % count, blk)
    before = ((space + count - 1) % count, blk)
    layers = x_ref.shape[0]
    half = layers // 2

    def at(dz=0, dx=0, block=None):
        return (((z + dz + nz) % nz) * NXC + (x + dx) % NXC, blk if block is None else block)

    group = [at(0, g // GROUP, base + (b4 + g % GROUP) % GROUP) for g in range(1, NXC * GROUP)]
    rings = [at(dz) for dz in (-BOX, -2, -1, 1, 2, BOX)]

    copies = []

    def push(src, dst, device):
        index = len(copies)
        copy = pltpu.make_async_remote_copy(
            src_ref=src,
            dst_ref=dst,
            send_sem=send.at[index],
            recv_sem=recv.at[index],
            device_id=device,
            device_id_type=MESH,
        )
        copy.start()
        copies.append(copy)
        return copy

    def landed(*some):
        for copy in some:
            copy.wait_recv()

    barrier = pltpu.get_barrier_semaphore()
    peers = group + rings + [after, before]
    for device in peers:
        pl.semaphore_signal(barrier, inc=1, device_id=device, device_id_type=MESH)
    there, here = (1 - high) * half, high * half
    rows = x_ref.shape[1]
    side = rows // 16
    row = lax.broadcasted_iota(jnp.int32, (rows, WIDTH), 0)
    pos_y, pos_z = row // 16, row % 16

    def flag(cond):
        return jnp.where(cond, 1.0, 0.0)

    lowest, highest = flag(space > 0), flag(space < count - 1)
    plane = flag(pos_y > 0) + flag(pos_y < side - 1) + flag(pos_z > 0) + flag(pos_z < 15)
    zero16 = jnp.zeros((16, WIDTH), F32)

    def image(i, up, down, deg_x):
        cur = x_ref[i]
        near = up + down
        near = near + jnp.concatenate([cur[16:], zero16], axis=0)
        near = near + jnp.concatenate([zero16, cur[:-16]], axis=0)
        near = near + jnp.where(pos_z < 15, pltpu.roll(cur, rows - 1, 0), 0.0)
        near = near + jnp.where(pos_z > 0, pltpu.roll(cur, 1, 0), 0.0)
        value = cur + ((plane + deg_x) * cur - near)
        w[i] = value
        wh[i], wl[i] = halves(value)

    @pl.loop(1, layers - 1)
    def _(i):
        image(i, x_ref[i + 1], x_ref[i - 1], 2.0)

    def chunk(c):
        out_half[c] = jnp.where(high == 0, w[there + c], x_ref[there + c])
        return push(out_half.at[c], in_half.at[c], peer_y)

    pl.semaphore_wait(barrier, len(peers))
    chunks = [chunk(c) for c in range(half - 1)]
    halos = [push(x_ref.at[layers - 1], halo.at[0], after), push(x_ref.at[0], halo.at[1], before)]
    whole = push(x_ref, xp, core)

    @pl.loop(0, layers)
    def _(i):
        xh[i], xl[i] = halves(x_ref[i])

    landed(*halos)
    image(0, x_ref[1], jnp.where(space > 0, halo[0], 0.0), 1.0 + lowest)
    image(layers - 1, jnp.where(space < count - 1, halo[1], 0.0), x_ref[layers - 2], 1.0 + highest)
    chunks.append(chunk(half - 1))
    images = push(w.at[pl.ds(here, half)], wp, core)

    landed(whole)

    def gram_own(i, total):
        ph, plow = halves(xp[i])
        xph[i], xpl[i] = ph, plow
        right = (jnp.concatenate([xh[i], ph], axis=1), jnp.concatenate([xl[i], plow], axis=1))
        return total + dot3((wh[i], wl[i]), right, ROWS_IN)

    gram = lax.fori_loop(0, layers, gram_own, jnp.zeros((WIDTH, 2 * WIDTH), F32))
    ga, rxa, sa, rza, ringa, ta, gza, fa = bufs_a
    gb, rxb, sb, rzb, ringb, tb, gzb, fb = bufs_b
    for t in range(WIDTH // 8):
        ga[t // BOX, t % BOX, 0] = gram[8 * t : 8 * t + 8, :WIDTH]
        ga[t // BOX, t % BOX, 1] = gram[8 * t : 8 * t + 8, WIDTH:]

    def over_x(src, dst):
        return [push(src.at[(x + d) % NXC], dst.at[d - 1], at(0, d)) for d in range(1, NXC)]

    def over_z(src, dst):
        return [push(src.at[(z + o + nz) % BOX], dst.at[j], at(o)) for j, o in enumerate(Z_IN)]

    def ring_step(k, own, slots, boxes):
        up = boxes // 2
        out = [push(own if k == 0 else slots.at[k - 1], slots.at[k], at(BOX))]
        if k < boxes - 1 - up:
            out.append(push(own if k == 0 else slots.at[up + k - 1], slots.at[up + k], at(-BOX)))
        return out

    def back_z(src, dst):
        return [push(src, dst.at[z % BOX], at(o)) for o in Z_OUT]

    boxes = nz // BOX

    a_x = over_x(ga, rxa)
    landed(images)
    cross_own = jnp.zeros((WIDTH, WIDTH), F32)
    cross_peer = jnp.zeros((WIDTH, WIDTH), F32)
    a_z = None
    a_r = None
    for c in range(half):
        landed(chunks[c])
        right = halves(in_half[c])
        own_left = halves(jnp.where(high == 0, w[here + c], x_ref[here + c]))
        peer_left = halves(jnp.where(high == 0, wp[c], xp[here + c]))
        cross_own = cross_own + dot3(own_left, right, ROWS_IN)
        cross_peer = cross_peer + dot3(peer_left, right, ROWS_IN)
        if c == 0:
            landed(*a_x)
            sa[...] = ga[x] + rxa[0] + rxa[1] + rxa[2]
            a_z = over_z(sa, rza)
        if c == half - 2:
            landed(*a_z)
            ta[...] = sa[z % BOX] + rza[0] + rza[1] + rza[2]
            a_r = ring_step(0, ta, ringa, boxes)
    keep = jnp.where(high == 0, cross_own, cross_peer.T)
    give = jnp.where(high == 0, cross_peer, cross_own.T)
    for t in range(WIDTH // 8):
        gb[t // BOX, t % BOX] = keep[8 * t : 8 * t + 8]
        keep_give[t // BOX, t % BOX] = give[8 * t : 8 * t + 8]
    owner = base + (1 - high) * (3 - b4) + high * (b4 - 2)
    b_x = over_x(gb, rxb)
    b_x += [push(keep_give.at[(x + d) % NXC], rxb.at[3 + d], at(0, d, owner)) for d in range(NXC)]

    steps = boxes // 2
    landed(*a_r)
    a_r = ring_step(1, ta, ringa, boxes)
    landed(*b_x)
    total = gb[x]
    for j in range(7):
        total = total + rxb[j]
    sb[...] = total
    b_z = over_z(sb, rzb)
    rest = push(x_ref, xq, peer_y)
    landed(*a_r)
    a_r = ring_step(2, ta, ringa, boxes)
    landed(*b_z)
    tb[...] = sb[z % BOX] + rzb[0] + rzb[1] + rzb[2]
    up, far = boxes // 2, 2 * BOX
    b_far = [push(tb, ringb.at[1], at(far)), push(tb, ringb.at[up + 1], at(-far))]
    b_r = [push(tb, ringb.at[0], at(BOX)), push(tb, ringb.at[up], at(-BOX))]
    landed(*a_r)
    a_r = ring_step(3, ta, ringa, boxes)
    landed(*a_r)
    total = ta[...]
    for j in range(boxes - 1):
        total = total + ringa[j]
    gza[z % BOX] = total
    a_g = back_z(gza.at[z % BOX], gza)
    landed(*b_far)
    b_r.append(push(ringb.at[1], ringb.at[3], at(far)))
    b_r.append(push(ringb.at[1], ringb.at[2], at(BOX)))
    b_r.append(push(ringb.at[up + 1], ringb.at[up + 2], at(-BOX)))
    landed(*a_g)
    fa[x] = gza[...]
    a_g = [push(fa.at[x], fa.at[x], at(0, d)) for d in range(1, NXC)]
    landed(*a_g)
    a_c = push(fa, core_a, core)
    landed(*b_r)
    total = tb[...]
    for j in range(boxes - 1):
        total = total + ringb[j]
    gzb[z % BOX] = total
    b_g = back_z(gzb.at[z % BOX], gzb)
    landed(a_c)
    square = (WIDTH, WIDTH)
    own_a, own_c = fa[:, :, 0].reshape(square), fa[:, :, 1].reshape(square)
    peer_a, peer_c = core_a[:, :, 0].reshape(square), core_a[:, :, 1].reshape(square)
    eye = eye_mask()

    def column(values):
        return jnp.sum(jnp.where(eye, values, 0.0), axis=1, keepdims=True)

    def diag_row(values):
        return jnp.sum(jnp.where(eye, values, 0.0), axis=0, keepdims=True)

    spread, moved = [], []

    def serve(step):
        if step == 6:
            landed(*b_g)
            fb[b4, x] = gzb[...]
            spread.extend(push(fb.at[b4, x], fb.at[b4, x], device) for device in group)
        if step == 11:
            landed(rest)
            moved.append(push(xq, xq1, core))

    sign = jnp.where(low == 1, 1.0, -1.0)
    keep_m, take_m = rotation(column(own_a), diag_row(peer_a), own_c, sign, serve)
    pair = jnp.concatenate([keep_m, take_m], axis=0)
    kt[...] = pair
    turn = push(kt, ktq, peer_y)
    full = jnp.concatenate(
        [jnp.concatenate([own_a, own_c], axis=1), jnp.concatenate([peer_c, peer_a], axis=1)], axis=0
    )
    own_diag = jnp.sum(pair * mul(full, pair), axis=0, keepdims=True)
    dg[...] = jnp.broadcast_to(own_diag, (8, WIDTH))
    turn_d = push(dg, dgq, peer_y)

    def wide(pair):
        ph, plow = halves(pair)
        return jnp.concatenate([ph, plow], axis=1), ph

    def mixed(lh, ll, right):
        both, ph = right
        part = lax.dot_general(lh, both, ROWS_OUT, preferred_element_type=F32)
        last = lax.dot_general(ll, ph, ROWS_OUT, preferred_element_type=F32)
        return part[:, :WIDTH] + (part[:, WIDTH:] + last)

    own_wide = wide(pair)
    landed(turn)
    pair_q = ktq[...]
    peer_wide = wide(pair_q)
    landed(*spread)
    top = jnp.concatenate([fb[low].reshape(square), fb[2 + low].reshape(square)], axis=1)
    bottom = jnp.concatenate([fb[3 - low].reshape(square), fb[1 - low].reshape(square)], axis=1)
    cross = jnp.concatenate([top, bottom], axis=0)
    left = jnp.where(high == 0, pair, pair_q)
    right = jnp.where(high == 0, pair_q, pair)
    turned = mul(left, mul(cross, right), ROWS_IN)
    turned = jnp.where(high == 0, turned, turned.T)
    landed(*moved, turn_d)
    diag_q = dgq[:1]

    def first_round(step):
        i = step // 2
        if step % 2 == 0:
            lh = jnp.concatenate([xh[i], xph[i]], axis=1)
            ll = jnp.concatenate([xl[i], xpl[i]], axis=1)
            first_h[i, :, :WIDTH], first_l[i, :, :WIDTH] = halves(mixed(lh, ll, own_wide))
        else:
            qh, ql = halves(xq[i])
            q1h, q1l = halves(xq1[i])
            lh, ll = jnp.concatenate([qh, q1h], axis=1), jnp.concatenate([ql, q1l], axis=1)
            first_h[i, :, WIDTH:], first_l[i, :, WIDTH:] = halves(mixed(lh, ll, peer_wide))

    sign = jnp.where(high == 1, 1.0, -1.0)
    keep_m, take_m = rotation(column(own_diag), diag_q, turned, sign, first_round)
    last_wide = wide(jnp.concatenate([keep_m, take_m], axis=0))

    @pl.loop(0, layers)
    def _(i):
        out_ref[i] = mixed(first_h[i], first_l[i], last_wide)

    for copy in copies:
        copy.wait_send()


def rotate(block):
    nz = lax.axis_size("space") // NXC
    layers, rows, _ = block.shape
    half = layers // 2
    boxes = nz // BOX
    full = pltpu.VMEM((layers, rows, WIDTH), F32)
    part = pltpu.VMEM((layers, rows, WIDTH), BF16)
    double = pltpu.VMEM((layers, rows, 2 * WIDTH), BF16)

    def sums(arrivals, trail, blocks):
        return [
            pltpu.VMEM((NXC, BOX) + trail, F32),
            pltpu.VMEM((arrivals, BOX) + trail, F32),
            pltpu.VMEM((BOX,) + trail, F32),
            pltpu.VMEM((3,) + trail, F32),
            pltpu.VMEM((boxes - 1,) + trail, F32),
            pltpu.VMEM(trail, F32),
            pltpu.VMEM((BOX,) + trail, F32),
            pltpu.VMEM(blocks + (NXC, BOX) + trail, F32),
        ]

    trail_a, trail_b = (2, 8, WIDTH), (8, WIDTH)
    return pl.pallas_call(
        functools.partial(kernel, nz),
        out_shape=jax.ShapeDtypeStruct(block.shape, F32),
        in_specs=[pl.BlockSpec(memory_space=pltpu.VMEM)],
        out_specs=pl.BlockSpec(memory_space=pltpu.VMEM),
        scratch_shapes=[
            full,
            full,
            full,
            pltpu.VMEM((2, rows, WIDTH), F32),
            full,
            pltpu.VMEM((half, rows, WIDTH), F32),
            pltpu.VMEM((half, rows, WIDTH), F32),
            pltpu.VMEM((half, rows, WIDTH), F32),
            part,
            part,
            part,
            part,
            part,
            part,
            double,
            double,
            sums(3, trail_a, ()),
            sums(7, trail_b, (GROUP,)),
            pltpu.VMEM((NXC, BOX) + trail_a, F32),
            pltpu.VMEM((NXC, BOX) + trail_b, F32),
            pltpu.VMEM((2 * WIDTH, WIDTH), F32),
            pltpu.VMEM((2 * WIDTH, WIDTH), F32),
            pltpu.VMEM((8, WIDTH), F32),
            pltpu.VMEM((8, WIDTH), F32),
            pltpu.SemaphoreType.DMA((80,)),
            pltpu.SemaphoreType.DMA((80,)),
        ],
        compiler_params=pltpu.CompilerParams(
            collective_id=0, has_side_effects=True, vmem_limit_bytes=48 * 1024 * 1024
        ),
    )(block)


def shards(snapshots):
    layers, cells_y, cells_z, width = snapshots.shape
    return rotate(snapshots.reshape(layers, cells_y * cells_z, width)).reshape(snapshots.shape)


def solution(mesh):
    return jax.shard_map(
        shards,
        mesh=mesh,
        in_specs=(P("space", None, None, "blk"),),
        out_specs=P("space", None, None, "blk"),
        check_vma=False,
    )
```

```python
import functools

import jax
import jax.numpy as jnp
from jax import lax
from jax.experimental import pallas as pl
from jax.experimental.pallas import tpu as pltpu
from jax.sharding import PartitionSpec as P

NXC = 4
GROUP = 4
BOX = 4
WIDTH = 128
F32, BF16 = jnp.float32, jnp.bfloat16
MESH = pl.DeviceIdType.MESH
ROWS_IN, ROWS_OUT = (((0,), (0,)), ((), ())), (((1,), (0,)), ((), ()))
LANES = (((1,), (1,)), ((), ()))
Z_IN = (-2, -1, 1)
Z_OUT = (-1, 1, 2)


def halves(value):
    high = value.astype(BF16)
    return high, (value - high.astype(F32)).astype(BF16)


def dot3(left, right, dims=ROWS_OUT):
    (lh, ll), (rh, rl) = left, right

    def dot(u, v):
        return lax.dot_general(u, v, dims, preferred_element_type=F32)

    return dot(lh, rh) + (dot(lh, rl) + dot(ll, rh))


def mul(left, right, dims=ROWS_OUT):
    return dot3(halves(left), halves(right), dims)


def eye_mask():
    shape = (WIDTH, WIDTH)
    return lax.broadcasted_iota(jnp.int32, shape, 0) == lax.broadcasted_iota(jnp.int32, shape, 1)


def inverse_of(matrix, between):
    count = WIDTH // 8
    shape = (8, WIDTH)
    panels = [matrix[8 * i : 8 * i + 8] for i in range(count)]
    lane = lax.broadcasted_iota(jnp.int32, shape, 1)
    sub = lax.broadcasted_iota(jnp.int32, shape, 0)
    for home in range(count):
        first = 8 * home
        rows = [jnp.broadcast_to(panels[home][t : t + 1], shape) for t in range(8)]
        entry = [[None] * 8 for _ in range(8)]
        for t in range(8):
            for u in range(t, 8):
                place = rows[t][:, first + u : first + u + 1]
                entry[t][u] = entry[u][t] = jnp.broadcast_to(place, shape)
        block = (lane >= first) & (lane < first + 8)
        for t in range(8):
            rows[t] = jnp.where(block, jnp.where(lane == first + t, 1.0, 0.0), rows[t])
        for t in range(8):
            pivot = 1.0 / entry[t][t]
            rows[t] = rows[t] * pivot
            for v in range(t + 1, 8):
                entry[t][v] = entry[t][v] * pivot
            for u in range(8):
                if u != t:
                    rows[u] = rows[u] - entry[u][t] * rows[t]
                    for v in range(t + 1, 8):
                        entry[u][v] = entry[u][v] - entry[u][t] * entry[t][v]
        for i in range(count):
            old = panels[i]
            if i == home:
                new = rows[0]
                for t in range(1, 8):
                    new = jnp.where(sub == t, rows[t], new)
            else:
                new = jnp.where(block, 0.0, old)
                for t in range(8):
                    new = new - old[:, first + t : first + t + 1] * rows[t]
            panels[i] = new
        between(home)
    return jnp.concatenate(panels, axis=0)


def rotation(own_col, peer_row, cross, parity, between):
    eye = jnp.where(eye_mask(), 1.0, 0.0)
    ratios = cross / (own_col + peer_row)
    inverse = inverse_of(eye + mul(ratios, ratios, LANES), between)
    solved = mul(inverse, ratios)
    return 2.0 * inverse - eye, (2.0 * parity) * solved.T


def kernel(nz, x_hbm, out_ref, x_ref, xp, xq, xq1, halo, w, wp, out_half, in_half, xh, xl, xph, xpl, wh, wl, first_h, first_l, bufs_a, bufs_b, core_a, keep_give, kt, ktq, send, recv):
    space, blk = lax.axis_index("space"), lax.axis_index("blk")
    count = nz * NXC
    z, x = space // NXC, space % NXC
    b4 = blk % GROUP
    base, low, high = blk - b4, b4 % 2, b4 // 2
    core = (space, base + 2 * high + 1 - low)
    peer_y = (space, base + (b4 + 2) % GROUP)
    after = ((space + 1) % count, blk)
    before = ((space + count - 1) % count, blk)
    layers = x_ref.shape[0]
    half = layers // 2

    def at(dz=0, dx=0, block=None):
        return (((z + dz + nz) % nz) * NXC + (x + dx) % NXC, blk if block is None else block)

    group = [at(0, g // GROUP, base + (b4 + g % GROUP) % GROUP) for g in range(1, NXC * GROUP)]
    rings = [at(dz) for dz in (-BOX, -2, -1, 1, 2, BOX)]

    copies = []

    def push(src, dst, device):
        index = len(copies)
        copy = pltpu.make_async_remote_copy(
            src_ref=src,
            dst_ref=dst,
            send_sem=send.at[index],
            recv_sem=recv.at[index],
            device_id=device,
            device_id_type=MESH,
        )
        copy.start()
        copies.append(copy)
        return copy

    def landed(*some):
        for copy in some:
            copy.wait_recv()

    load = pltpu.make_async_copy(x_hbm, x_ref, recv.at[79])
    load.start()
    barrier = pltpu.get_barrier_semaphore()
    peers = group + rings + [after, before]
    for device in peers:
        pl.semaphore_signal(barrier, inc=1, device_id=device, device_id_type=MESH)
    load.wait()
    there, here = (1 - high) * half, high * half
    rows = x_ref.shape[1]
    side = rows // 16
    row = lax.broadcasted_iota(jnp.int32, (rows, WIDTH), 0)
    pos_y, pos_z = row // 16, row % 16

    def flag(cond):
        return jnp.where(cond, 1.0, 0.0)

    lowest, highest = flag(space > 0), flag(space < count - 1)
    plane = flag(pos_y > 0) + flag(pos_y < side - 1) + flag(pos_z > 0) + flag(pos_z < 15)
    zero16 = jnp.zeros((16, WIDTH), F32)

    def image(i, up, down, deg_x):
        cur = x_ref[i]
        near = up + down
        near = near + jnp.concatenate([cur[16:], zero16], axis=0)
        near = near + jnp.concatenate([zero16, cur[:-16]], axis=0)
        near = near + jnp.where(pos_z < 15, pltpu.roll(cur, rows - 1, 0), 0.0)
        near = near + jnp.where(pos_z > 0, pltpu.roll(cur, 1, 0), 0.0)
        value = cur + ((plane + deg_x) * cur - near)
        w[i] = value
        wh[i], wl[i] = halves(value)

    @pl.loop(1, layers - 1)
    def _(i):
        image(i, x_ref[i + 1], x_ref[i - 1], 2.0)

    def chunk(c):
        out_half[c] = jnp.where(high == 0, w[there + c], x_ref[there + c])
        return push(out_half.at[c], in_half.at[c], peer_y)

    pl.semaphore_wait(barrier, len(peers))
    chunks = [chunk(c) for c in range(half - 1)]
    halos = [push(x_ref.at[layers - 1], halo.at[0], after), push(x_ref.at[0], halo.at[1], before)]
    whole = push(x_ref, xp, core)

    @pl.loop(0, layers)
    def _(i):
        xh[i], xl[i] = halves(x_ref[i])

    landed(*halos)
    image(0, x_ref[1], jnp.where(space > 0, halo[0], 0.0), 1.0 + lowest)
    image(layers - 1, jnp.where(space < count - 1, halo[1], 0.0), x_ref[layers - 2], 1.0 + highest)
    chunks.append(chunk(half - 1))
    images = push(w.at[pl.ds(here, half)], wp, core)

    landed(whole)

    def gram_own(i, total):
        ph, plow = halves(xp[i])
        xph[i], xpl[i] = ph, plow
        right = (jnp.concatenate([xh[i], ph], axis=1), jnp.concatenate([xl[i], plow], axis=1))
        return total + dot3((wh[i], wl[i]), right, ROWS_IN)

    gram = lax.fori_loop(0, layers, gram_own, jnp.zeros((WIDTH, 2 * WIDTH), F32))
    ga, rxa, sa, rza, ringa, ta, gza, fa = bufs_a
    gb, rxb, sb, rzb, ringb, tb, gzb, fb = bufs_b
    for t in range(WIDTH // 8):
        ga[t // BOX, t % BOX, 0] = gram[8 * t : 8 * t + 8, :WIDTH]
        ga[t // BOX, t % BOX, 1] = gram[8 * t : 8 * t + 8, WIDTH:]

    def over_x(src, dst):
        return [push(src.at[(x + d) % NXC], dst.at[d - 1], at(0, d)) for d in range(1, NXC)]

    def over_z(src, dst):
        return [push(src.at[(z + o + nz) % BOX], dst.at[j], at(o)) for j, o in enumerate(Z_IN)]

    def ring_step(k, own, slots, boxes):
        up = boxes // 2
        out = [push(own if k == 0 else slots.at[k - 1], slots.at[k], at(BOX))]
        if k < boxes - 1 - up:
            out.append(push(own if k == 0 else slots.at[up + k - 1], slots.at[up + k], at(-BOX)))
        return out

    def back_z(src, dst):
        return [push(src, dst.at[z % BOX], at(o)) for o in Z_OUT]

    boxes = nz // BOX

    a_x = over_x(ga, rxa)
    landed(images)
    cross_own = jnp.zeros((WIDTH, WIDTH), F32)
    cross_peer = jnp.zeros((WIDTH, WIDTH), F32)
    a_z = None
    a_r = None
    for c in range(half):
        landed(chunks[c])
        right = halves(in_half[c])
        own_left = halves(jnp.where(high == 0, w[here + c], x_ref[here + c]))
        peer_left = halves(jnp.where(high == 0, wp[c], xp[here + c]))
        cross_own = cross_own + dot3(own_left, right, ROWS_IN)
        cross_peer = cross_peer + dot3(peer_left, right, ROWS_IN)
        if c == 0:
            landed(*a_x)
            sa[...] = ga[x] + rxa[0] + rxa[1] + rxa[2]
            a_z = over_z(sa, rza)
        if c == half - 2:
            landed(*a_z)
            ta[...] = sa[z % BOX] + rza[0] + rza[1] + rza[2]
            a_r = ring_step(0, ta, ringa, boxes)
    keep = jnp.where(high == 0, cross_own, cross_peer.T)
    give = jnp.where(high == 0, cross_peer, cross_own.T)
    for t in range(WIDTH // 8):
        gb[t // BOX, t % BOX] = keep[8 * t : 8 * t + 8]
        keep_give[t // BOX, t % BOX] = give[8 * t : 8 * t + 8]
    owner = base + (1 - high) * (3 - b4) + high * (b4 - 2)
    b_x = over_x(gb, rxb)
    b_x += [push(keep_give.at[(x + d) % NXC], rxb.at[3 + d], at(0, d, owner)) for d in range(NXC)]
    rest = push(x_ref, xq, peer_y)

    steps = boxes // 2
    landed(*a_r)
    a_r = ring_step(1, ta, ringa, boxes)
    landed(*b_x)
    total = gb[x]
    for j in range(7):
        total = total + rxb[j]
    sb[...] = total
    b_z = over_z(sb, rzb)
    landed(*a_r)
    a_r = ring_step(2, ta, ringa, boxes)
    landed(*b_z)
    tb[...] = sb[z % BOX] + rzb[0] + rzb[1] + rzb[2]
    b_r = ring_step(0, tb, ringb, boxes)
    landed(*a_r)
    a_r = ring_step(3, ta, ringa, boxes)
    landed(*b_r)
    b_r = ring_step(1, tb, ringb, boxes)
    landed(*a_r)
    total = ta[...]
    for j in range(boxes - 1):
        total = total + ringa[j]
    gza[z % BOX] = total
    a_g = back_z(gza.at[z % BOX], gza)
    landed(*b_r)
    b_r = ring_step(2, tb, ringb, boxes)
    landed(*a_g)
    fa[x] = gza[...]
    a_g = [push(fa.at[x], fa.at[x], at(0, d)) for d in range(1, NXC)]
    landed(*b_r)
    b_r = ring_step(3, tb, ringb, boxes)
    landed(*a_g)
    a_c = push(fa, core_a, core)
    landed(*b_r)
    total = tb[...]
    for j in range(boxes - 1):
        total = total + ringb[j]
    gzb[z % BOX] = total
    b_g = back_z(gzb.at[z % BOX], gzb)
    landed(a_c)
    square = (WIDTH, WIDTH)
    own_a, own_c = fa[:, :, 0].reshape(square), fa[:, :, 1].reshape(square)
    peer_a, peer_c = core_a[:, :, 0].reshape(square), core_a[:, :, 1].reshape(square)
    eye = eye_mask()

    def column(values):
        return jnp.sum(jnp.where(eye, values, 0.0), axis=1, keepdims=True)

    def diag_row(values):
        return jnp.sum(jnp.where(eye, values, 0.0), axis=0, keepdims=True)

    spread, moved = [], []

    def serve(step):
        if step == 6:
            landed(*b_g)
            fb[b4, x] = gzb[...]
            spread.extend(push(fb.at[b4, x], fb.at[b4, x], device) for device in group)
        if step == 11:
            landed(rest)
            moved.append(push(xq, xq1, core))

    sign = jnp.where(low == 1, 1.0, -1.0)
    keep_m, take_m = rotation(column(own_a), diag_row(peer_a), own_c, sign, serve)
    pair = jnp.concatenate([keep_m, take_m], axis=0)
    full = jnp.concatenate(
        [jnp.concatenate([own_a, own_c], axis=1), jnp.concatenate([peer_c, peer_a], axis=1)], axis=0
    )
    own_diag = jnp.sum(pair * mul(full, pair), axis=0, keepdims=True)
    kt[: 2 * WIDTH] = pair
    kt[2 * WIDTH :] = jnp.broadcast_to(own_diag, (8, WIDTH))
    turn = push(kt, ktq, peer_y)

    def wide(pair):
        ph, plow = halves(pair)
        return jnp.concatenate([ph, plow], axis=1), ph

    def mixed(lh, ll, right):
        both, ph = right
        part = lax.dot_general(lh, both, ROWS_OUT, preferred_element_type=F32)
        last = lax.dot_general(ll, ph, ROWS_OUT, preferred_element_type=F32)
        return part[:, :WIDTH] + (part[:, WIDTH:] + last)

    own_wide = wide(pair)
    landed(turn)
    pair_q = ktq[: 2 * WIDTH]
    diag_q = ktq[2 * WIDTH : 2 * WIDTH + 1]
    peer_wide = wide(pair_q)
    landed(*spread)
    top = jnp.concatenate([fb[low].reshape(square), fb[2 + low].reshape(square)], axis=1)
    bottom = jnp.concatenate([fb[3 - low].reshape(square), fb[1 - low].reshape(square)], axis=1)
    cross = jnp.concatenate([top, bottom], axis=0)
    left = jnp.where(high == 0, pair, pair_q)
    right = jnp.where(high == 0, pair_q, pair)
    turned = mul(left, mul(cross, right), ROWS_IN)
    turned = jnp.where(high == 0, turned, turned.T)
    landed(*moved)

    def first_round(step):
        i = step // 2
        if step % 2 == 0:
            lh = jnp.concatenate([xh[i], xph[i]], axis=1)
            ll = jnp.concatenate([xl[i], xpl[i]], axis=1)
            first_h[i, :, :WIDTH], first_l[i, :, :WIDTH] = halves(mixed(lh, ll, own_wide))
        else:
            qh, ql = halves(xq[i])
            q1h, q1l = halves(xq1[i])
            lh, ll = jnp.concatenate([qh, q1h], axis=1), jnp.concatenate([ql, q1l], axis=1)
            first_h[i, :, WIDTH:], first_l[i, :, WIDTH:] = halves(mixed(lh, ll, peer_wide))

    sign = jnp.where(high == 1, 1.0, -1.0)
    keep_m, take_m = rotation(column(own_diag), diag_q, turned, sign, first_round)
    last_wide = wide(jnp.concatenate([keep_m, take_m], axis=0))

    @pl.loop(0, layers)
    def _(i):
        out_ref[i] = mixed(first_h[i], first_l[i], last_wide)

    for copy in copies:
        copy.wait_send()


def rotate(block):
    nz = lax.axis_size("space") // NXC
    layers, rows, _ = block.shape
    half = layers // 2
    boxes = nz // BOX
    full = pltpu.VMEM((layers, rows, WIDTH), F32)
    part = pltpu.VMEM((layers, rows, WIDTH), BF16)
    double = pltpu.VMEM((layers, rows, 2 * WIDTH), BF16)

    def sums(arrivals, trail, blocks):
        return [
            pltpu.VMEM((NXC, BOX) + trail, F32),
            pltpu.VMEM((arrivals, BOX) + trail, F32),
            pltpu.VMEM((BOX,) + trail, F32),
            pltpu.VMEM((3,) + trail, F32),
            pltpu.VMEM((boxes - 1,) + trail, F32),
            pltpu.VMEM(trail, F32),
            pltpu.VMEM((BOX,) + trail, F32),
            pltpu.VMEM(blocks + (NXC, BOX) + trail, F32),
        ]

    trail_a, trail_b = (2, 8, WIDTH), (8, WIDTH)
    return pl.pallas_call(
        functools.partial(kernel, nz),
        out_shape=jax.ShapeDtypeStruct(block.shape, F32),
        in_specs=[pl.BlockSpec(memory_space=pl.ANY)],
        out_specs=pl.BlockSpec(memory_space=pltpu.VMEM),
        scratch_shapes=[
            full,
            full,
            full,
            full,
            pltpu.VMEM((2, rows, WIDTH), F32),
            full,
            pltpu.VMEM((half, rows, WIDTH), F32),
            pltpu.VMEM((half, rows, WIDTH), F32),
            pltpu.VMEM((half, rows, WIDTH), F32),
            part,
            part,
            part,
            part,
            part,
            part,
            double,
            double,
            sums(3, trail_a, ()),
            sums(7, trail_b, (GROUP,)),
            pltpu.VMEM((NXC, BOX) + trail_a, F32),
            pltpu.VMEM((NXC, BOX) + trail_b, F32),
            pltpu.VMEM((2 * WIDTH + 8, WIDTH), F32),
            pltpu.VMEM((2 * WIDTH + 8, WIDTH), F32),
            pltpu.SemaphoreType.DMA((80,)),
            pltpu.SemaphoreType.DMA((80,)),
        ],
        compiler_params=pltpu.CompilerParams(
            collective_id=0, has_side_effects=True, vmem_limit_bytes=48 * 1024 * 1024
        ),
    )(block)


def shards(snapshots):
    layers, cells_y, cells_z, width = snapshots.shape
    return rotate(snapshots.reshape(layers, cells_y * cells_z, width)).reshape(snapshots.shape)


def solution(mesh):
    return jax.shard_map(
        shards,
        mesh=mesh,
        in_specs=(P("space", None, None, "blk"),),
        out_specs=P("space", None, None, "blk"),
        check_vma=False,
    )
```
